512 devices in a mesh: group: 16 (over x_lo, y, core), shard: 32 (over x_hi, z).
Axes of the slice: x: 4 (x_hi: 2, x_lo: 2; x = x_hi * 2 + x_lo), y: 4, z: 16, core: 2. Of those that a mesh axis runs over, the one named last changes fastest.
Arguments:
- patches: bfloat16 [3, 1024, 5120], P(None, ('group', 'shard')), may hold values from -24 to 24
- image_lengths: int32 [3, 4], replicated, may hold values from 1 to 512, 1024 in all within a row
- destination: int32 [3, 16], replicated, may hold values from 0 to 15, each once within a row
- query_key_value_weight: bfloat16 [5120, 32, 384], P('group', 'shard'), may hold values from -0.078125 to 0.078125
Outputs:
- attended: bfloat16 [3, 1024, 32, 128], P(None, 'group', 'shard')
The draws below stay inside these ranges and needn't reach their ends.
All inputs are finite; a program needn't handle non-finite values.
Results may differ from the reference program's by a relative error of at most 0.012.
The reference program's roundings to bfloat16 on the way (of `rows`, `proj` and `weights`) count: a program that leaves them out, or rounds other values in their place, can miss the bound.
Values may be sent and summed in bfloat16 or wider, within the bound.
No kernel may reach another device: no remote copies, remote signals or barrier semaphores. Data moves between devices by JAX's collectives and lax.ppermute only.
A program may use at most 64 MiB of HBM per device.

```python
import math
import jax
import jax.numpy as jnp
import numpy as np
from jax import lax

D = 5120
HD = 128
BLK = 64
NPACK = 3
IMGS = 4
HEADS = 32
LEN = 1024
MOST = 512
N_GROUP = 16


def draw_patches(key, part):
    key = jax.random.fold_in(key, 11)
    first_key = jax.random.fold_in(key, 0)
    base = jax.random.normal(first_key, (NPACK, LEN, D), jnp.float32)
    return jnp.clip(base, -6.0, 6.0).astype(jnp.bfloat16)


def block_levels(stream_key, shape, cuts, least, largest):
    loudness, own = 1.0, jax.random.fold_in(stream_key, 6)
    for axis_at, parts in cuts:
        heights = jnp.exp(jax.random.uniform(jax.random.fold_in(own, axis_at), (parts,), jnp.float32, least / len(cuts), largest / len(cuts)))
        loudness = loudness * jnp.repeat(heights, shape[axis_at] // parts).reshape([-1 if axis == axis_at else 1 for axis in range(len(shape))])
    return loudness


def split_up(amount, total, most, lean):
    weights = [(1 << 20) // math.isqrt(standing ** lean) + 1 for standing in range(2, amount + 1)]
    spare, given = total - most - (amount - 1), [1] * (amount - 1)
    while spare > 0:
        movable = [i for i in range(amount - 1) if given[i] < most]
        pool, remaining = sum([weights[i] for i in movable]), spare
        for i in movable:
            addition = min(most - given[i], max(1, remaining * weights[i] // pool), spare)
            given[i] = given[i] + addition
            spare = spare - addition
    return np.array([most] + given)


def ragged_sizes(stream_key, count, total, limit, lean):
    if count == 2:
        one = jax.random.randint(stream_key, (), max(1, total - limit), min(limit, total - 1) + 1)
        return jnp.stack([one, total - one])
    sizes = jnp.asarray(split_up(count, total, limit, lean), jnp.int32)
    twos = (count - 1) // 2
    giver, taker = sizes[1:1 + 2 * twos:2], sizes[2:2 + 2 * twos:2]
    room = jnp.minimum(giver - 1, limit - taker)
    moved = jax.random.randint(jax.random.fold_in(stream_key, 1), (twos,), 0, 1 << 20) % (room + 1)
    sizes = sizes.at[1:1 + 2 * twos:2].set(giver - moved).at[2:2 + 2 * twos:2].set(taker + moved)
    return sizes[jax.random.permutation(jax.random.fold_in(stream_key, 2), count)]


def normal_values(rng, extent, spread, most, cuts=(), kind=jnp.bfloat16):
    drawn = jax.random.normal(rng, extent, jnp.float32) * spread
    if len(cuts) > 0:
        drawn = block_levels(rng, extent, cuts, -0.22, 0.18) * drawn
    return jnp.clip(drawn, min=-most, max=most).astype(kind)


def setup_inputs(seed: int = 0) -> dict:
    splits = jax.random.split(jax.random.key(seed), 5)
    return {
        "patches": draw_patches(jax.random.fold_in(splits[4], 71), 0),
        "image_lengths": jax.vmap(lambda own: ragged_sizes(own, IMGS, LEN, MOST, 2))(jax.random.split(splits[1], NPACK)).reshape((NPACK, IMGS)).astype(jnp.int32),
        "destination": jax.vmap(lambda own: jax.random.permutation(own, N_GROUP))(jax.random.split(splits[2], NPACK)).reshape((NPACK, N_GROUP)).astype(jnp.int32),
        "query_key_value_weight": normal_values(splits[3], (D, HEADS, 3 * HD), D ** -0.5, 0.078125, ((0, 16), (1, 32))),
    }


def reference(patches, image_lengths, destination, query_key_value_weight):
    weight_mat = query_key_value_weight.reshape(D, HEADS * 3 * HD)
    positions = jnp.arange(LEN, dtype=jnp.int32)
    score_scale = HD ** -0.5
    source_block = jnp.argsort(destination, axis=1).astype(jnp.int32)
    blocks = patches.reshape(NPACK, N_GROUP, BLK, D)
    rows = jnp.take_along_axis(blocks, source_block[:, :, None, None], axis=1).reshape(NPACK, LEN, D)

    def one_pack(pack_items):
        pack_rows, pack_lengths = pack_items
        image_ends = jnp.cumsum(pack_lengths)
        segment = jnp.sum((positions[:, None] >= image_ends[None, :]).astype(jnp.int32), axis=1)
        proj = jnp.dot(pack_rows, weight_mat, preferred_element_type=jnp.float32)
        proj = proj.astype(jnp.bfloat16).reshape(LEN, HEADS, 3, HD).astype(jnp.float32)
        query_matrix = proj[:, :, 0]
        projected_key_rows = proj[:, :, 1]
        projected_value_rows = proj[:, :, 2]
        scores = jnp.einsum("qhc,khc->hqk", query_matrix, projected_key_rows) * score_scale
        same_image = segment[:, None] == segment[None, :]
        scores = jnp.where(same_image[None], scores, -jnp.inf)
        row_max = jnp.max(scores, axis=-1, keepdims=True)
        attention_probabilities = jnp.exp(scores - row_max)
        attention_probabilities = (attention_probabilities / jnp.sum(attention_probabilities, axis=-1, keepdims=True)).astype(jnp.bfloat16)
        attention_output = jnp.einsum("hqk,khc->qhc", attention_probabilities.astype(jnp.float32), projected_value_rows)
        return attention_output.astype(jnp.bfloat16)

    return lax.map(one_pack, (rows, image_lengths))
```

```python
import jax
import jax.numpy as jnp
from jax import lax
from jax.experimental import pallas as pl
from jax.experimental.pallas import tpu as pltpu
from jax.sharding import Mesh, PartitionSpec as P

D = 5120
HD = 128
BLK = 64
HALF = BLK // 2
NPACK = 3
IMGS = 4
NBLK = 16
QKV = 3 * HD
SENT = 5 * HD
NZ = 16
PIECE = D // 16
KSET = 4 * PIECE
LOCAL = NPACK * 2
ROWS = NPACK * BLK

FINE = (("xl", 2), ("y", 4), ("c", 2), ("xh", 2), ("z", 16))
GROUP = ("xl", "y", "c")
SHARD = ("xh", "z")
PACK_OF = (0, 1, 2, 2)
VMEM_BYTES = 32 * 2**20


def spread_kernel(w_ref, out_ref, sems):
    copies = [pltpu.make_async_copy(w_ref, out_ref.at[m], sems.at[m]) for m in range(8)]
    for copy in copies:
        copy.start()
    for copy in copies:
        copy.wait()


def column_kernel(x_ref, out_ref):
    own_xl, own_c = lax.axis_index("xl") == 1, lax.axis_index("c") == 1
    x = x_ref[...].astype(jnp.float32)
    x = jnp.where(own_xl, x[..., D // 2 :], x[..., : D // 2])
    x = jnp.concatenate([x[k, p] for k in range(4) for p in range(NPACK)], axis=0)
    cut = [
        jnp.where(own_c, x[:, (2 * y + 1) * PIECE : (2 * y + 2) * PIECE], x[:, 2 * y * PIECE : (2 * y + 1) * PIECE])
        for y in range(4)
    ]
    out_ref[...] = jnp.concatenate(cut, axis=1).astype(jnp.bfloat16)


def split(product):
    whole_part = product.astype(jnp.bfloat16)
    scored = slice(0, 2 * HD)
    rest = (product[:, scored] - whole_part[:, scored].astype(jnp.float32)).astype(jnp.bfloat16)
    return whole_part, rest


def joined(sent):
    scored = sent[:, : 2 * HD].astype(jnp.float32) + sent[:, QKV:].astype(jnp.float32)
    return scored, sent[:, 2 * HD : QKV].astype(jnp.float32)


def project_kernel(x_ref, w_ref, keep_ref, give_ref, product_ref):
    own = lax.axis_index("c")
    for head in range(2):
        product = jnp.dot(
            x_ref[...], w_ref[:, head].reshape(KSET, QKV), preferred_element_type=jnp.float32
        )
        for k in range(3):
            product_ref[k] = product[:, k * HD : (k + 1) * HD]
            columns = slice(head * QKV + k * HD, head * QKV + (k + 1) * HD)
            sent = slice(head * SENT + k * HD, head * SENT + (k + 1) * HD)
            remainder = slice(head * SENT + QKV + k * HD, head * SENT + QKV + (k + 1) * HD)
            for p in range(NPACK):
                for xl in range(2):
                    for i in range(2):
                        at = p * BLK + xl * HALF + i * NZ
                        first = xl * 2 * LOCAL + p * 2 + i
                        mine = product_ref[k, pl.ds(first + own * LOCAL, NZ, stride=4 * LOCAL), :]
                        theirs = product_ref[k, pl.ds(first + (1 - own) * LOCAL, NZ, stride=4 * LOCAL), :]
                        keep_ref[at : at + NZ, columns] = mine
                        rounded = theirs.astype(jnp.bfloat16)
                        give_ref[at : at + NZ, sent] = rounded
                        if k < 2:
                            rest = theirs - rounded.astype(jnp.float32)
                            give_ref[at : at + NZ, remainder] = rest.astype(jnp.bfloat16)


def pair_kernel(keep_ref, got_ref, out_ref):
    other = 1 - lax.axis_index("c")
    for p in range(NPACK):
        rows = slice(p * BLK, (p + 1) * BLK)
        for head in range(2):
            scored, value = joined(got_ref[other, rows, head * SENT : (head + 1) * SENT])
            total = keep_ref[rows, head * QKV : (head + 1) * QKV]
            total = jnp.concatenate([total[:, : 2 * HD] + scored, total[:, 2 * HD :] + value], axis=1)
            rounded, rest = split(total)
            for y, pack in enumerate(PACK_OF):
                if pack == p:
                    for xl in range(2):
                        out_ref[xl * 8 + y * 2 + head, :, :QKV] = rounded
                        out_ref[xl * 8 + y * 2 + head, :, QKV:] = rest


def total_kernel(parts_ref, out_ref):
    for y in range(4):
        for xh in range(2):
            at = y * 2 + xh
            scored, value = joined(parts_ref[at])
            more_scored, more_value = joined(parts_ref[8 + at])
            scored = (scored + more_scored).astype(jnp.bfloat16)
            value = (value + more_value).astype(jnp.bfloat16)
            for xl in range(2):
                block, half = slice(xl * HALF, (xl + 1) * HALF), slice(xh * HALF, (xh + 1) * HALF)
                out_ref[xl * 4 + y, half, : 2 * HD] = scored[block]
                out_ref[xl * 4 + y, half, 2 * HD :] = value[block]


def row_of(at):
    return (at & HALF) + ((at & (NZ - 1)) << 1) + ((at >> 4) & 1)


def attend_kernel(destination_ref, lengths_ref, qkv_ref, out_ref, ordered_ref):
    xl, y_own, c = (lax.axis_index(a) for a in ("xl", "y", "c"))
    pack = jnp.minimum(y_own, NPACK - 1)
    ends = []
    end = 0
    for i in range(IMGS):
        end = end + lengths_ref[pack, i]
        ends.append(end)

    def segment(position):
        count = jnp.zeros(position.shape, jnp.int32)
        for e in ends:
            count = count + (position >= e).astype(jnp.int32)
        return count

    lane = lax.broadcasted_iota(jnp.int32, (1, NBLK * BLK), 1)
    key_block = jnp.zeros_like(lane)
    slots = []
    for j in range(NBLK):
        slot = (j & 1) * 8 + (j >> 1)
        slots.append(slot)
        key_block = jnp.where((lane >> 6) == slot, destination_ref[pack, j], key_block)
    key_ids = segment(key_block * BLK + row_of(lane))

    queries = []
    for y in range(4):
        block = xl * 8 + y * 2 + c
        start = 0
        for j in range(NBLK):
            start = jnp.where(destination_ref[pack, j] == block, slots[j] * BLK, start)
        start = pl.multiple_of(start, BLK)
        queries.append(qkv_ref[pl.ds(start, BLK), 0:HD])
    query = jnp.concatenate(queries, axis=0)
    row = lax.broadcasted_iota(jnp.int32, (4 * BLK, 1), 0)
    query_ids = segment((xl * 8 + c) * BLK + (row >> 6) * (2 * BLK) + row_of(row))

    scores = lax.dot_general(
        query,
        qkv_ref[:, HD : 2 * HD],
        (((1,), (1,)), ((), ())),
        preferred_element_type=jnp.float32,
    ) * (HD**-0.5)
    scores = jnp.where(query_ids == key_ids, scores, -jnp.inf)
    weights = jnp.exp(scores - jnp.max(scores, axis=-1, keepdims=True))
    weights = (weights * (1.0 / jnp.sum(weights, axis=-1, keepdims=True))).astype(jnp.bfloat16)
    attended = jnp.dot(weights, qkv_ref[:, 2 * HD : 3 * HD], preferred_element_type=jnp.float32)
    for at in range(0, 4 * BLK, NZ):
        first = at // HALF * HALF + (at // NZ) % 2
        ordered_ref[pl.ds(first, NZ, stride=2), :] = attended[at : at + NZ]
    for y in range(4):
        out_ref[y] = ordered_ref[y * BLK : (y + 1) * BLK].astype(jnp.bfloat16)


def whole(memory=pltpu.VMEM):
    return pl.BlockSpec(memory_space=memory)


def call(kernel, out, in_specs, scratch=(), cost=(0, 10**6, 0), out_specs=None):
    flops, bytes_accessed, transcendentals = cost
    return pl.pallas_call(
        kernel,
        out_shape=out,
        in_specs=in_specs,
        out_specs=out_specs or jax.tree.map(lambda _: whole(), out),
        scratch_shapes=list(scratch),
        compiler_params=pltpu.CompilerParams(vmem_limit_bytes=VMEM_BYTES),
        cost_estimate=pl.CostEstimate(
            flops=flops, bytes_accessed=bytes_accessed, transcendentals=transcendentals
        ),
    )


def shards(patches, image_lengths, destination, weight):
    half_type = jnp.bfloat16

    slots = call(
        spread_kernel,
        jax.ShapeDtypeStruct((8, PIECE, QKV), half_type),
        [whole(pl.ANY)],
        [pltpu.SemaphoreType.DMA((8,))],
        out_specs=whole(pl.ANY),
    )(weight.reshape(PIECE, QKV))
    near = lax.all_gather(patches, ("xl", "c"), axis=0)
    slots, near = lax.optimization_barrier((slots, near))
    weight_set = lax.all_to_all(slots, ("y", "xh"), 0, 0, tiled=True)

    rows = call(
        column_kernel, jax.ShapeDtypeStruct((4 * LOCAL, KSET), half_type), [whole()]
    )(near)
    rows = lax.all_gather(rows, "z", axis=0, tiled=True)

    keep, give = call(
        project_kernel,
        (
            jax.ShapeDtypeStruct((ROWS, 2 * QKV), jnp.float32),
            jax.ShapeDtypeStruct((ROWS, 2 * SENT), half_type),
        ),
        [whole(), whole()],
        [pltpu.VMEM((3, 4 * LOCAL * NZ, HD), jnp.float32)],
        cost=(10**9, 4 * 10**6, 0),
    )(rows, weight_set.reshape(4, 2, PIECE, QKV))

    got = lax.all_gather(give, "c", axis=0)
    spread = call(
        pair_kernel,
        jax.ShapeDtypeStruct((16, BLK, SENT), half_type),
        [whole(), whole()],
    )(keep, got)
    parts = lax.all_to_all(spread, ("xl", "y", "xh"), 0, 0, tiled=True)
    blocks = call(total_kernel, jax.ShapeDtypeStruct((8, BLK, QKV), half_type), [whole()])(parts)
    blocks = lax.all_gather(blocks.reshape(8 * BLK, QKV), "c", axis=0, tiled=True)

    attended = call(
        attend_kernel,
        jax.ShapeDtypeStruct((4, BLK, HD), half_type),
        [whole(pltpu.SMEM)] * 2 + [whole()],
        [pltpu.VMEM((4 * BLK, HD), jnp.float32)],
        cost=(2 * 10**8, 10**6, 3 * 10**5),
    )(destination, image_lengths, blocks)

    home = lax.all_to_all(attended, "y", 0, 0, tiled=True)
    return home[:NPACK].reshape(NPACK, BLK, 1, HD)


def solution(mesh):
    names, sizes = zip(*FINE)
    fine = Mesh(mesh.devices.reshape(sizes), names)
    return jax.shard_map(
        shards,
        mesh=fine,
        in_specs=(P(None, GROUP + SHARD, None), P(), P(), P(GROUP, SHARD, None)),
        out_specs=P(None, GROUP, SHARD, None),
        check_vma=False,
    )
```

```python
import jax
import jax.numpy as jnp
from jax import lax
from jax.experimental import pallas as pl
from jax.experimental.pallas import tpu as pltpu
from jax.sharding import Mesh, PartitionSpec as P

D = 5120
HD = 128
BLK = 64
HALF = BLK // 2
NPACK = 3
IMGS = 4
NBLK = 16
QKV = 3 * HD
SENT = 5 * HD
NZ = 16
PIECE = D // 16
KSET = 4 * PIECE
LOCAL = NPACK * 2
ROWS = NPACK * BLK

FINE = (("xl", 2), ("y", 4), ("c", 2), ("xh", 2), ("z", 16))
GROUP = ("xl", "y", "c")
SHARD = ("xh", "z")
PACK_OF = (0, 1, 2, 2)
VMEM_BYTES = 32 * 2**20


def spread_kernel(w_ref, out_ref, sems):
    copies = [pltpu.make_async_copy(w_ref, out_ref.at[m], sems.at[m]) for m in range(8)]
    for copy in copies:
        copy.start()
    for copy in copies:
        copy.wait()


def column_kernel(x_ref, out_ref):
    own_xl, own_c = lax.axis_index("xl") == 1, lax.axis_index("c") == 1
    x = x_ref[...].astype(jnp.float32)
    x = jnp.where(own_xl, x[..., D // 2 :], x[..., : D // 2])
    x = jnp.concatenate([x[k, p] for k in range(4) for p in range(NPACK)], axis=0)
    cut = [
        jnp.where(own_c, x[:, (2 * y + 1) * PIECE : (2 * y + 2) * PIECE], x[:, 2 * y * PIECE : (2 * y + 1) * PIECE])
        for y in range(4)
    ]
    out_ref[...] = jnp.concatenate(cut, axis=1).astype(jnp.bfloat16)


def split(product):
    whole_part = product.astype(jnp.bfloat16)
    scored = slice(0, 2 * HD)
    rest = (product[:, scored] - whole_part[:, scored].astype(jnp.float32)).astype(jnp.bfloat16)
    return whole_part, rest


def joined(sent):
    scored = sent[:, : 2 * HD].astype(jnp.float32) + sent[:, QKV:].astype(jnp.float32)
    return scored, sent[:, 2 * HD : QKV].astype(jnp.float32)


def project_kernel(x_ref, w_ref, keep_ref, give_ref, product_ref):
    own = lax.axis_index("c")
    for head in range(2):
        product = jnp.dot(
            x_ref[...], w_ref[:, head].reshape(KSET, QKV), preferred_element_type=jnp.float32
        )
        for k in range(3):
            product_ref[k] = product[:, k * HD : (k + 1) * HD]
            columns = slice(head * QKV + k * HD, head * QKV + (k + 1) * HD)
            sent = slice(head * SENT + k * HD, head * SENT + (k + 1) * HD)
            remainder = slice(head * SENT + QKV + k * HD, head * SENT + QKV + (k + 1) * HD)
            for p in range(NPACK):
                for xl in range(2):
                    for i in range(2):
                        at = p * BLK + xl * HALF + i * NZ
                        first = xl * 2 * LOCAL + p * 2 + i
                        mine = product_ref[k, pl.ds(first + own * LOCAL, NZ, stride=4 * LOCAL), :]
                        theirs = product_ref[k, pl.ds(first + (1 - own) * LOCAL, NZ, stride=4 * LOCAL), :]
                        keep_ref[at : at + NZ, columns] = mine
                        rounded = theirs.astype(jnp.bfloat16)
                        give_ref[at : at + NZ, sent] = rounded
                        if k < 2:
                            rest = theirs - rounded.astype(jnp.float32)
                            give_ref[at : at + NZ, remainder] = rest.astype(jnp.bfloat16)


def pair_kernel(keep_ref, got_ref, out_ref):
    other = 1 - lax.axis_index("c")
    for p in range(NPACK):
        rows = slice(p * BLK, (p + 1) * BLK)
        for head in range(2):
            scored, value = joined(got_ref[other, rows, head * SENT : (head + 1) * SENT])
            total = keep_ref[rows, head * QKV : (head + 1) * QKV]
            total = jnp.concatenate([total[:, : 2 * HD] + scored, total[:, 2 * HD :] + value], axis=1)
            rounded, rest = split(total)
            for xl in range(2):
                block, at = slice(xl * HALF, (xl + 1) * HALF), slice(p * HALF, (p + 1) * HALF)
                out_ref[xl * 2 + head, at, :QKV] = rounded[block]
                out_ref[xl * 2 + head, at, QKV:] = rest[block]


def total_kernel(parts_ref, out_ref):
    for p in range(NPACK):
        at = slice(p * HALF, (p + 1) * HALF)
        for xh in range(2):
            scored, value = joined(parts_ref[xh, at])
            more_scored, more_value = joined(parts_ref[2 + xh, at])
            scored = (scored + more_scored).astype(jnp.bfloat16)
            value = (value + more_value).astype(jnp.bfloat16)
            half = slice(xh * HALF, (xh + 1) * HALF)
            for y, pack in enumerate(PACK_OF):
                if pack == p:
                    for xl in range(2):
                        out_ref[xl * 4 + y, half, : 2 * HD] = scored
                        out_ref[xl * 4 + y, half, 2 * HD :] = value


def row_of(at):
    return (at & HALF) + ((at & (NZ - 1)) << 1) + ((at >> 4) & 1)


def attend_kernel(destination_ref, lengths_ref, qkv_ref, out_ref, ordered_ref):
    xl, y_own, c = (lax.axis_index(a) for a in ("xl", "y", "c"))
    pack = jnp.minimum(y_own, NPACK - 1)
    ends = []
    end = 0
    for i in range(IMGS):
        end = end + lengths_ref[pack, i]
        ends.append(end)

    def segment(position):
        count = jnp.zeros(position.shape, jnp.int32)
        for e in ends:
            count = count + (position >= e).astype(jnp.int32)
        return count

    lane = lax.broadcasted_iota(jnp.int32, (1, NBLK * BLK), 1)
    key_block = jnp.zeros_like(lane)
    slots = []
    for j in range(NBLK):
        slot = (j & 1) * 8 + (j >> 1)
        slots.append(slot)
        key_block = jnp.where((lane >> 6) == slot, destination_ref[pack, j], key_block)
    key_ids = segment(key_block * BLK + row_of(lane))

    queries = []
    for y in range(4):
        block = xl * 8 + y * 2 + c
        start = 0
        for j in range(NBLK):
            start = jnp.where(destination_ref[pack, j] == block, slots[j] * BLK, start)
        start = pl.multiple_of(start, BLK)
        queries.append(qkv_ref[pl.ds(start, BLK), 0:HD])
    query = jnp.concatenate(queries, axis=0)
    row = lax.broadcasted_iota(jnp.int32, (4 * BLK, 1), 0)
    query_ids = segment((xl * 8 + c) * BLK + (row >> 6) * (2 * BLK) + row_of(row))

    scores = lax.dot_general(
        query,
        qkv_ref[:, HD : 2 * HD],
        (((1,), (1,)), ((), ())),
        preferred_element_type=jnp.float32,
    ) * (HD**-0.5)
    scores = jnp.where(query_ids == key_ids, scores, -jnp.inf)
    weights = jnp.exp(scores - jnp.max(scores, axis=-1, keepdims=True))
    weights = (weights * (1.0 / jnp.sum(weights, axis=-1, keepdims=True))).astype(jnp.bfloat16)
    attended = jnp.dot(weights, qkv_ref[:, 2 * HD : 3 * HD], preferred_element_type=jnp.float32)
    for at in range(0, 4 * BLK, NZ):
        first = at // HALF * HALF + (at // NZ) % 2
        ordered_ref[pl.ds(first, NZ, stride=2), :] = attended[at : at + NZ]
    for y in range(4):
        out_ref[y] = ordered_ref[y * BLK : (y + 1) * BLK].astype(jnp.bfloat16)


def whole(memory=pltpu.VMEM):
    return pl.BlockSpec(memory_space=memory)


def call(kernel, out, in_specs, scratch=(), cost=(0, 10**6, 0), out_specs=None):
    flops, bytes_accessed, transcendentals = cost
    return pl.pallas_call(
        kernel,
        out_shape=out,
        in_specs=in_specs,
        out_specs=out_specs or jax.tree.map(lambda _: whole(), out),
        scratch_shapes=list(scratch),
        compiler_params=pltpu.CompilerParams(vmem_limit_bytes=VMEM_BYTES),
        cost_estimate=pl.CostEstimate(
            flops=flops, bytes_accessed=bytes_accessed, transcendentals=transcendentals
        ),
    )


def shards(patches, image_lengths, destination, weight):
    half_type = jnp.bfloat16

    slots = call(
        spread_kernel,
        jax.ShapeDtypeStruct((8, PIECE, QKV), half_type),
        [whole(pl.ANY)],
        [pltpu.SemaphoreType.DMA((8,))],
        out_specs=whole(pl.ANY),
    )(weight.reshape(PIECE, QKV))
    near = lax.all_gather(patches, ("xl", "c"), axis=0)
    slots, near = lax.optimization_barrier((slots, near))
    weight_set = lax.all_to_all(slots, ("y", "xh"), 0, 0, tiled=True)

    rows = call(
        column_kernel, jax.ShapeDtypeStruct((4 * LOCAL, KSET), half_type), [whole()]
    )(near)
    rows = lax.all_gather(rows, "z", axis=0, tiled=True)

    keep, give = call(
        project_kernel,
        (
            jax.ShapeDtypeStruct((ROWS, 2 * QKV), jnp.float32),
            jax.ShapeDtypeStruct((ROWS, 2 * SENT), half_type),
        ),
        [whole(), whole()],
        [pltpu.VMEM((3, 4 * LOCAL * NZ, HD), jnp.float32)],
        cost=(10**9, 4 * 10**6, 0),
    )(rows, weight_set.reshape(4, 2, PIECE, QKV))

    got = lax.all_gather(give, "c", axis=0)
    spread = call(
        pair_kernel,
        jax.ShapeDtypeStruct((4, NPACK * HALF, SENT), half_type),
        [whole(), whole()],
    )(keep, got)
    parts = lax.all_to_all(spread, ("xl", "xh"), 0, 0, tiled=True)
    spread = call(total_kernel, jax.ShapeDtypeStruct((8, BLK, QKV), half_type), [whole()])(parts)
    blocks = lax.all_to_all(spread, ("xl", "y"), 0, 0, tiled=True)
    blocks = lax.all_gather(blocks.reshape(8 * BLK, QKV), "c", axis=0, tiled=True)

    attended = call(
        attend_kernel,
        jax.ShapeDtypeStruct((4, BLK, HD), half_type),
        [whole(pltpu.SMEM)] * 2 + [whole()],
        [pltpu.VMEM((4 * BLK, HD), jnp.float32)],
        cost=(2 * 10**8, 10**6, 3 * 10**5),
    )(destination, image_lengths, blocks)

    home = lax.all_to_all(attended, "y", 0, 0, tiled=True)
    return home[:NPACK].reshape(NPACK, BLK, 1, HD)


def solution(mesh):
    names, sizes = zip(*FINE)
    fine = Mesh(mesh.devices.reshape(sizes), names)
    return jax.shard_map(
        shards,
        mesh=fine,
        in_specs=(P(None, GROUP + SHARD, None), P(), P(), P(GROUP, SHARD, None)),
        out_specs=P(None, GROUP, SHARD, None),
        check_vma=False,
    )
```

```python
import jax
import jax.numpy as jnp
from jax import lax
from jax.experimental import pallas as pl
from jax.experimental.pallas import tpu as pltpu
from jax.sharding import Mesh, PartitionSpec as P

D = 5120
HD = 128
BLK = 64
HALF = BLK // 2
NPACK = 3
IMGS = 4
NBLK = 16
QKV = 3 * HD
SENT = 5 * HD
NZ = 16
PIECE = D // 16
KSET = 4 * PIECE
LOCAL = NPACK * 2
ROWS = NPACK * BLK

FINE = (("xl", 2), ("y", 4), ("c", 2), ("xh", 2), ("z", 16))
GROUP = ("xl", "y", "c")
SHARD = ("xh", "z")
PACK_OF = (0, 1, 2, 2)
VMEM_BYTES = 32 * 2**20


def spread_kernel(w_ref, out_ref, sems):
    copies = [pltpu.make_async_copy(w_ref, out_ref.at[m], sems.at[m]) for m in range(8)]
    for copy in copies:
        copy.start()
    for copy in copies:
        copy.wait()


def column_kernel(x_ref, out_ref):
    own_xl, own_c = lax.axis_index("xl") == 1, lax.axis_index("c") == 1
    x = x_ref[...].astype(jnp.float32)
    x = jnp.where(own_xl, x[..., D // 2 :], x[..., : D // 2])
    x = jnp.concatenate([x[k, p] for k in range(4) for p in range(NPACK)], axis=0)
    cut = [
        jnp.where(own_c, x[:, (2 * y + 1) * PIECE : (2 * y + 2) * PIECE], x[:, 2 * y * PIECE : (2 * y + 1) * PIECE])
        for y in range(4)
    ]
    out_ref[...] = jnp.concatenate(cut, axis=1).astype(jnp.bfloat16)


def split(product):
    whole_part = product.astype(jnp.bfloat16)
    scored = slice(0, 2 * HD)
    rest = (product[:, scored] - whole_part[:, scored].astype(jnp.float32)).astype(jnp.bfloat16)
    return whole_part, rest


def joined(sent):
    scored = sent[:, : 2 * HD].astype(jnp.float32) + sent[:, QKV:].astype(jnp.float32)
    return scored, sent[:, 2 * HD : QKV].astype(jnp.float32)


def project_kernel(x_ref, w_ref, keep_ref, give_ref, product_ref):
    own = lax.axis_index("c")
    for head in range(2):
        product = jnp.dot(
            x_ref[...], w_ref[:, head].reshape(KSET, QKV), preferred_element_type=jnp.float32
        )
        for k in range(3):
            product_ref[k, : 4 * LOCAL * NZ] = product[:, k * HD : (k + 1) * HD]
            columns = slice(head * QKV + k * HD, head * QKV + (k + 1) * HD)
            sent = slice(head * SENT + k * HD, head * SENT + (k + 1) * HD)
            remainder = slice(head * SENT + QKV + k * HD, head * SENT + QKV + (k + 1) * HD)
            for p in range(NPACK):
                for xl in range(2):
                    for i in range(2):
                        at = p * BLK + xl * HALF + i * NZ
                        first = xl * 2 * LOCAL + p * 2 + i
                        mine = product_ref[k, pl.ds(first + own * LOCAL, NZ, stride=4 * LOCAL), :]
                        theirs = product_ref[k, pl.ds(first + (1 - own) * LOCAL, NZ, stride=4 * LOCAL), :]
                        keep_ref[at : at + NZ, columns] = mine
                        rounded = theirs.astype(jnp.bfloat16)
                        give_ref[at : at + NZ, sent] = rounded
                        if k < 2:
                            rest = theirs - rounded.astype(jnp.float32)
                            give_ref[at : at + NZ, remainder] = rest.astype(jnp.bfloat16)


def pair_kernel(keep_ref, got_ref, out_ref):
    other = 1 - lax.axis_index("c")
    for p in range(NPACK):
        rows = slice(p * BLK, (p + 1) * BLK)
        for head in range(2):
            scored, value = joined(got_ref[other, rows, head * SENT : (head + 1) * SENT])
            total = keep_ref[rows, head * QKV : (head + 1) * QKV]
            total = jnp.concatenate([total[:, : 2 * HD] + scored, total[:, 2 * HD :] + value], axis=1)
            rounded, rest = split(total)
            for xl in range(2):
                block, at = slice(xl * HALF, (xl + 1) * HALF), slice(p * HALF, (p + 1) * HALF)
                out_ref[xl * 2 + head, at, :QKV] = rounded[block]
                out_ref[xl * 2 + head, at, QKV:] = rest[block]


def total_kernel(parts_ref, out_ref):
    for p in range(NPACK):
        at = slice(p * HALF, (p + 1) * HALF)
        for xh in range(2):
            scored, value = joined(parts_ref[xh, at])
            more_scored, more_value = joined(parts_ref[2 + xh, at])
            scored = (scored + more_scored).astype(jnp.bfloat16)
            value = (value + more_value).astype(jnp.bfloat16)
            half = slice(xh * HALF, (xh + 1) * HALF)
            for y, pack in enumerate(PACK_OF):
                if pack == p:
                    for xl in range(2):
                        out_ref[xl * 4 + y, half, : 2 * HD] = scored
                        out_ref[xl * 4 + y, half, 2 * HD :] = value


def row_of(at):
    return (at & HALF) + ((at & (NZ - 1)) << 1) + ((at >> 4) & 1)


def attend_kernel(destination_ref, lengths_ref, qkv_ref, out_ref, ordered_ref):
    xl, y_own, c = (lax.axis_index(a) for a in ("xl", "y", "c"))
    pack = jnp.minimum(y_own, NPACK - 1)
    ends = []
    end = 0
    for i in range(IMGS):
        end = end + lengths_ref[pack, i]
        ends.append(end)

    def segment(position):
        count = jnp.zeros(position.shape, jnp.int32)
        for e in ends:
            count = count + (position >= e).astype(jnp.int32)
        return count

    lane = lax.broadcasted_iota(jnp.int32, (1, NBLK * BLK), 1)
    key_block = jnp.zeros_like(lane)
    slots = []
    for j in range(NBLK):
        slot = (j & 1) * 8 + (j >> 1)
        slots.append(slot)
        key_block = jnp.where((lane >> 6) == slot, destination_ref[pack, j], key_block)
    key_ids = segment(key_block * BLK + row_of(lane))

    queries = []
    for y in range(4):
        block = xl * 8 + y * 2 + c
        start = 0
        for j in range(NBLK):
            start = jnp.where(destination_ref[pack, j] == block, slots[j] * BLK, start)
        start = pl.multiple_of(start, BLK)
        queries.append(qkv_ref[pl.ds(start, BLK), 0:HD])
    query = jnp.concatenate(queries, axis=0)
    row = lax.broadcasted_iota(jnp.int32, (4 * BLK, 1), 0)
    query_ids = segment((xl * 8 + c) * BLK + (row >> 6) * (2 * BLK) + row_of(row))

    scores = lax.dot_general(
        query,
        qkv_ref[:, HD : 2 * HD],
        (((1,), (1,)), ((), ())),
        preferred_element_type=jnp.float32,
    ) * (HD**-0.5)
    scores = jnp.where(query_ids == key_ids, scores, -jnp.inf)
    weights = jnp.exp(scores - jnp.max(scores, axis=-1, keepdims=True))
    weights = (weights * (1.0 / jnp.sum(weights, axis=-1, keepdims=True))).astype(jnp.bfloat16)
    attended = jnp.dot(weights, qkv_ref[:, 2 * HD : 3 * HD], preferred_element_type=jnp.float32)
    for at in range(0, 4 * BLK, NZ):
        first = at // HALF * HALF + (at // NZ) % 2
        ordered_ref[pl.ds(first, NZ, stride=2), :] = attended[at : at + NZ]
    for y in range(4):
        out_ref[y] = ordered_ref[y * BLK : (y + 1) * BLK].astype(jnp.bfloat16)


def whole(memory=pltpu.VMEM):
    return pl.BlockSpec(memory_space=memory)


def call(kernel, out, in_specs, scratch=(), cost=(0, 10**6, 0), out_specs=None):
    flops, bytes_accessed, transcendentals = cost
    return pl.pallas_call(
        kernel,
        out_shape=out,
        in_specs=in_specs,
        out_specs=out_specs or jax.tree.map(lambda _: whole(), out),
        scratch_shapes=list(scratch),
        compiler_params=pltpu.CompilerParams(vmem_limit_bytes=VMEM_BYTES),
        cost_estimate=pl.CostEstimate(
            flops=flops, bytes_accessed=bytes_accessed, transcendentals=transcendentals
        ),
    )


def shards(patches, image_lengths, destination, weight):
    half_type = jnp.bfloat16

    slots = call(
        spread_kernel,
        jax.ShapeDtypeStruct((8, PIECE, QKV), half_type),
        [whole(pl.ANY)],
        [pltpu.SemaphoreType.DMA((8,))],
        out_specs=whole(pl.ANY),
    )(weight.reshape(PIECE, QKV))
    near = lax.all_gather(patches, ("xl", "c"), axis=0)
    slots, near = lax.optimization_barrier((slots, near))
    weight_set = lax.all_to_all(slots, ("y", "xh"), 0, 0, tiled=True)

    rows = call(
        column_kernel, jax.ShapeDtypeStruct((4 * LOCAL, KSET), half_type), [whole()]
    )(near)
    rows = lax.all_gather(rows, "z", axis=0, tiled=True)

    keep, give = call(
        project_kernel,
        (
            jax.ShapeDtypeStruct((ROWS, 2 * QKV), jnp.float32),
            jax.ShapeDtypeStruct((ROWS, 2 * SENT), half_type),
        ),
        [whole(), whole()],
        [pltpu.VMEM((3, 4 * LOCAL * (NZ + 1), HD), jnp.float32)],
        cost=(10**9, 4 * 10**6, 0),
    )(rows, weight_set.reshape(4, 2, PIECE, QKV))

    got = lax.all_gather(give, "c", axis=0)
    spread = call(
        pair_kernel,
        jax.ShapeDtypeStruct((4, NPACK * HALF, SENT), half_type),
        [whole(), whole()],
    )(keep, got)
    parts = lax.all_to_all(spread, ("xl", "xh"), 0, 0, tiled=True)
    spread = call(total_kernel, jax.ShapeDtypeStruct((8, BLK, QKV), half_type), [whole()])(parts)
    blocks = lax.all_to_all(spread, ("xl", "y"), 0, 0, tiled=True)
    blocks = lax.all_gather(blocks.reshape(8 * BLK, QKV), "c", axis=0, tiled=True)

    attended = call(
        attend_kernel,
        jax.ShapeDtypeStruct((4, BLK, HD), half_type),
        [whole(pltpu.SMEM)] * 2 + [whole()],
        [pltpu.VMEM((4 * BLK + 8, HD), jnp.float32)],
        cost=(2 * 10**8, 10**6, 3 * 10**5),
    )(destination, image_lengths, blocks)

    home = lax.all_to_all(attended, "y", 0, 0, tiled=True)
    return home[:NPACK].reshape(NPACK, BLK, 1, HD)


def solution(mesh):
    names, sizes = zip(*FINE)
    fine = Mesh(mesh.devices.reshape(sizes), names)
    return jax.shard_map(
        shards,
        mesh=fine,
        in_specs=(P(None, GROUP + SHARD, None), P(), P(), P(GROUP, SHARD, None)),
        out_specs=P(None, GROUP, SHARD, None),
        check_vma=False,
    )
```

```python
import jax
import jax.numpy as jnp
from jax import lax
from jax.experimental import pallas as pl
from jax.experimental.pallas import tpu as pltpu
from jax.sharding import Mesh, PartitionSpec as P

D = 5120
HD = 128
BLK = 64
HALF = BLK // 2
NPACK = 3
IMGS = 4
NBLK = 16
QKV = 3 * HD
NZ = 16
PIECE = D // 16
KSET = 4 * PIECE
LOCAL = NPACK * 2
ROWS = NPACK * BLK

FINE = (("xl", 2), ("y", 4), ("c", 2), ("xh", 2), ("z", 16))
GROUP = ("xl", "y", "c")
SHARD = ("xh", "z")
PACK_OF = (0, 1, 2, 2)
VMEM_BYTES = 32 * 2**20


def spread_kernel(w_ref, out_ref, sems):
    copies = [pltpu.make_async_copy(w_ref, out_ref.at[m], sems.at[m]) for m in range(8)]
    for copy in copies:
        copy.start()
    for copy in copies:
        copy.wait()


def column_kernel(x_ref, out_ref):
    own_xl, own_c = lax.axis_index("xl") == 1, lax.axis_index("c") == 1
    x = x_ref[...].astype(jnp.float32)
    x = jnp.where(own_xl, x[..., D // 2 :], x[..., : D // 2])
    x = jnp.concatenate([x[k, p] for k in range(4) for p in range(NPACK)], axis=0)
    cut = [
        jnp.where(own_c, x[:, (2 * y + 1) * PIECE : (2 * y + 2) * PIECE], x[:, 2 * y * PIECE : (2 * y + 1) * PIECE])
        for y in range(4)
    ]
    out_ref[...] = jnp.concatenate(cut, axis=1).astype(jnp.bfloat16)


def project_kernel(x_ref, w_ref, keep_ref, give_ref, product_ref):
    own = lax.axis_index("c")
    for head in range(2):
        product = jnp.dot(
            x_ref[...], w_ref[:, head].reshape(KSET, QKV), preferred_element_type=jnp.float32
        )
        for k in range(3):
            product_ref[k, : 4 * LOCAL * NZ] = product[:, k * HD : (k + 1) * HD]
            columns = slice(head * QKV + k * HD, head * QKV + (k + 1) * HD)
            for p in range(NPACK):
                for xl in range(2):
                    for i in range(2):
                        at = p * BLK + xl * HALF + i * NZ
                        first = xl * 2 * LOCAL + p * 2 + i
                        mine = product_ref[k, pl.ds(first + own * LOCAL, NZ, stride=4 * LOCAL), :]
                        theirs = product_ref[k, pl.ds(first + (1 - own) * LOCAL, NZ, stride=4 * LOCAL), :]
                        keep_ref[at : at + NZ, columns] = mine
                        give_ref[at : at + NZ, columns] = theirs


def pair_kernel(keep_ref, got_ref, out_ref):
    for p in range(NPACK):
        for xl in range(2):
            start = p * BLK + xl * HALF
            for head in range(2):
                columns = slice(head * QKV, (head + 1) * QKV)
                total = keep_ref[start : start + HALF, columns] + got_ref[start : start + HALF, columns]
                out_ref[xl * 2 + head, p * HALF : (p + 1) * HALF] = total


def total_kernel(parts_ref, out_ref):
    for p in range(NPACK):
        at = slice(p * HALF, (p + 1) * HALF)
        for xh in range(2):
            total = (parts_ref[xh, at] + parts_ref[2 + xh, at]).astype(jnp.bfloat16)
            for y, pack in enumerate(PACK_OF):
                if pack == p:
                    for xl in range(2):
                        out_ref[xl * 4 + y, xh * HALF : (xh + 1) * HALF] = total


def row_of(at):
    return (at & HALF) + ((at & (NZ - 1)) << 1) + ((at >> 4) & 1)


def attend_kernel(destination_ref, lengths_ref, qkv_ref, out_ref, ordered_ref):
    xl, y_own, c = (lax.axis_index(a) for a in ("xl", "y", "c"))
    pack = jnp.minimum(y_own, NPACK - 1)
    ends = []
    end = 0
    for i in range(IMGS):
        end = end + lengths_ref[pack, i]
        ends.append(end)

    def segment(position):
        count = jnp.zeros(position.shape, jnp.int32)
        for e in ends:
            count = count + (position >= e).astype(jnp.int32)
        return count

    lane = lax.broadcasted_iota(jnp.int32, (1, NBLK * BLK), 1)
    key_block = jnp.zeros_like(lane)
    slots = []
    for j in range(NBLK):
        slot = (j & 1) * 8 + (j >> 1)
        slots.append(slot)
        key_block = jnp.where((lane >> 6) == slot, destination_ref[pack, j], key_block)
    key_ids = segment(key_block * BLK + row_of(lane))

    queries = []
    for y in range(4):
        block = xl * 8 + y * 2 + c
        start = 0
        for j in range(NBLK):
            start = jnp.where(destination_ref[pack, j] == block, slots[j] * BLK, start)
        start = pl.multiple_of(start, BLK)
        queries.append(qkv_ref[pl.ds(start, BLK), 0:HD])
    query = jnp.concatenate(queries, axis=0)
    row = lax.broadcasted_iota(jnp.int32, (4 * BLK, 1), 0)
    query_ids = segment((xl * 8 + c) * BLK + (row >> 6) * (2 * BLK) + row_of(row))

    scores = lax.dot_general(
        query,
        qkv_ref[:, HD : 2 * HD],
        (((1,), (1,)), ((), ())),
        preferred_element_type=jnp.float32,
    ) * (HD**-0.5)
    scores = jnp.where(query_ids == key_ids, scores, -jnp.inf)
    weights = jnp.exp(scores - jnp.max(scores, axis=-1, keepdims=True))
    weights = (weights * (1.0 / jnp.sum(weights, axis=-1, keepdims=True))).astype(jnp.bfloat16)
    attended = jnp.dot(weights, qkv_ref[:, 2 * HD : 3 * HD], preferred_element_type=jnp.float32)
    for at in range(0, 4 * BLK, NZ):
        first = at // HALF * HALF + (at // NZ) % 2
        ordered_ref[pl.ds(first, NZ, stride=2), :] = attended[at : at + NZ]
    for y in range(4):
        out_ref[y] = ordered_ref[y * BLK : (y + 1) * BLK].astype(jnp.bfloat16)


def whole(memory=pltpu.VMEM):
    return pl.BlockSpec(memory_space=memory)


def call(kernel, out, in_specs, scratch=(), cost=(0, 10**6, 0), out_specs=None):
    flops, bytes_accessed, transcendentals = cost
    return pl.pallas_call(
        kernel,
        out_shape=out,
        in_specs=in_specs,
        out_specs=out_specs or jax.tree.map(lambda _: whole(), out),
        scratch_shapes=list(scratch),
        compiler_params=pltpu.CompilerParams(vmem_limit_bytes=VMEM_BYTES),
        cost_estimate=pl.CostEstimate(
            flops=flops, bytes_accessed=bytes_accessed, transcendentals=transcendentals
        ),
    )


def shards(patches, image_lengths, destination, weight):
    half_type = jnp.bfloat16

    slots = call(
        spread_kernel,
        jax.ShapeDtypeStruct((8, PIECE, QKV), half_type),
        [whole(pl.ANY)],
        [pltpu.SemaphoreType.DMA((8,))],
        out_specs=whole(pl.ANY),
    )(weight.reshape(PIECE, QKV))
    near = lax.all_gather(patches, ("xl", "c"), axis=0)
    slots, near = lax.optimization_barrier((slots, near))
    weight_set = lax.all_to_all(slots, ("y", "xh"), 0, 0, tiled=True)

    rows = call(
        column_kernel, jax.ShapeDtypeStruct((4 * LOCAL, KSET), half_type), [whole()]
    )(near)
    rows = lax.all_gather(rows, "z", axis=0, tiled=True)

    keep, give = call(
        project_kernel,
        (
            jax.ShapeDtypeStruct((ROWS, 2 * QKV), jnp.float32),
            jax.ShapeDtypeStruct((ROWS, 2 * QKV), jnp.float32),
        ),
        [whole(), whole()],
        [pltpu.VMEM((3, 4 * LOCAL * (NZ + 1), HD), jnp.float32)],
        cost=(10**9, 4 * 10**6, 0),
    )(rows, weight_set.reshape(4, 2, PIECE, QKV))

    got = lax.ppermute(give, "c", [(0, 1), (1, 0)])
    spread = call(
        pair_kernel,
        jax.ShapeDtypeStruct((4, NPACK * HALF, QKV), jnp.float32),
        [whole(), whole()],
    )(keep, got)
    parts = lax.all_to_all(spread, ("xl", "xh"), 0, 0, tiled=True)
    spread = call(total_kernel, jax.ShapeDtypeStruct((8, BLK, QKV), half_type), [whole()])(parts)
    blocks = lax.all_to_all(spread, ("xl", "y"), 0, 0, tiled=True)
    blocks = lax.all_gather(blocks.reshape(8 * BLK, QKV), "c", axis=0, tiled=True)

    attended = call(
        attend_kernel,
        jax.ShapeDtypeStruct((4, BLK, HD), half_type),
        [whole(pltpu.SMEM)] * 2 + [whole()],
        [pltpu.VMEM((4 * BLK + 8, HD), jnp.float32)],
        cost=(2 * 10**8, 10**6, 3 * 10**5),
    )(destination, image_lengths, blocks)

    home = lax.all_to_all(attended, "y", 0, 0, tiled=True)
    return home[:NPACK].reshape(NPACK, BLK, 1, HD)


def solution(mesh):
    names, sizes = zip(*FINE)
    fine = Mesh(mesh.devices.reshape(sizes), names)
    return jax.shard_map(
        shards,
        mesh=fine,
        in_specs=(P(None, GROUP + SHARD, None), P(), P(), P(GROUP, SHARD, None)),
        out_specs=P(None, GROUP, SHARD, None),
        check_vma=False,
    )
```

```python
import jax
import jax.numpy as jnp
from jax import lax
from jax.experimental import pallas as pl
from jax.experimental.pallas import tpu as pltpu
from jax.sharding import Mesh, PartitionSpec as P

D = 5120
HD = 128
BLK = 64
HALF = BLK // 2
NPACK = 3
IMGS = 4
NBLK = 16
QKV = 3 * HD
NZ = 16
PIECE = D // 16
KSET = 4 * PIECE
LOCAL = NPACK * 2
ROWS = NPACK * BLK

FINE = (("xl", 2), ("y", 4), ("c", 2), ("xh", 2), ("z", 16))
GROUP = ("xl", "y", "c")
SHARD = ("xh", "z")
PACK_OF = (0, 1, 2, 2)
VMEM_BYTES = 32 * 2**20


def spread_kernel(w_ref, out_ref, sems):
    copies = [pltpu.make_async_copy(w_ref, out_ref.at[m], sems.at[m]) for m in range(8)]
    for copy in copies:
        copy.start()
    for copy in copies:
        copy.wait()


def column_kernel(x_ref, out_ref):
    own_xl, own_c = lax.axis_index("xl") == 1, lax.axis_index("c") == 1
    x = x_ref[...].astype(jnp.float32)
    x = jnp.where(own_xl, x[..., D // 2 :], x[..., : D // 2])
    x = jnp.concatenate([x[k, p] for k in range(4) for p in range(NPACK)], axis=0)
    cut = [
        jnp.where(own_c, x[:, (2 * y + 1) * PIECE : (2 * y + 2) * PIECE], x[:, 2 * y * PIECE : (2 * y + 1) * PIECE])
        for y in range(4)
    ]
    out_ref[...] = jnp.concatenate(cut, axis=1).astype(jnp.bfloat16)


def project_kernel(x_ref, w_ref, keep_ref, give_ref, product_ref):
    own = lax.axis_index("c")
    for head in range(2):
        product = jnp.dot(
            x_ref[...], w_ref[:, head].reshape(KSET, QKV), preferred_element_type=jnp.float32
        )
        for k in range(3):
            product_ref[k, : 4 * LOCAL * NZ] = product[:, k * HD : (k + 1) * HD]
            columns = slice(head * QKV + k * HD, head * QKV + (k + 1) * HD)
            for p in range(NPACK):
                for xl in range(2):
                    for i in range(2):
                        at = p * BLK + xl * HALF + i * NZ
                        first = xl * 2 * LOCAL + p * 2 + i
                        mine = product_ref[k, pl.ds(first + own * LOCAL, NZ, stride=4 * LOCAL), :]
                        theirs = product_ref[k, pl.ds(first + (1 - own) * LOCAL, NZ, stride=4 * LOCAL), :]
                        keep_ref[at : at + NZ, columns] = mine
                        give_ref[at : at + NZ, columns] = theirs


def pair_kernel(keep_ref, got_ref, out_ref):
    for p in range(NPACK):
        for xl in range(2):
            start = p * BLK + xl * HALF
            for head in range(2):
                columns = slice(head * QKV, (head + 1) * QKV)
                total = keep_ref[start : start + HALF, columns] + got_ref[start : start + HALF, columns]
                out_ref[xl * 2 + head, p * HALF : (p + 1) * HALF] = total


def total_kernel(parts_ref, out_ref):
    for p in range(NPACK):
        at = slice(p * HALF, (p + 1) * HALF)
        for xh in range(2):
            total = (parts_ref[xh, at] + parts_ref[2 + xh, at]).astype(jnp.bfloat16)
            for y, pack in enumerate(PACK_OF):
                if pack == p:
                    for xl in range(2):
                        out_ref[xl * 4 + y, xh * HALF : (xh + 1) * HALF] = total


def row_of(at):
    return (at & HALF) + ((at & (NZ - 1)) << 1) + ((at >> 4) & 1)


def mask_kernel(destination_ref, lengths_ref, bias_ref, start_ref):
    xl, y_own, c = (lax.axis_index(a) for a in ("xl", "y", "c"))
    pack = jnp.minimum(y_own, NPACK - 1)
    ends = []
    end = 0
    for i in range(IMGS):
        end = end + lengths_ref[pack, i]
        ends.append(end)

    def segment(position):
        count = jnp.zeros(position.shape, jnp.int32)
        for e in ends:
            count = count + (position >= e).astype(jnp.int32)
        return count

    lane = lax.broadcasted_iota(jnp.int32, (1, NBLK * BLK), 1)
    key_block = jnp.zeros_like(lane)
    slots = []
    for j in range(NBLK):
        slot = (j & 1) * 8 + (j >> 1)
        slots.append(slot)
        key_block = jnp.where((lane >> 6) == slot, destination_ref[pack, j], key_block)
    key_ids = segment(key_block * BLK + row_of(lane))

    for y in range(4):
        block = xl * 8 + y * 2 + c
        start = 0
        for j in range(NBLK):
            start = jnp.where(destination_ref[pack, j] == block, slots[j] * BLK, start)
        start_ref[y] = start
    row = lax.broadcasted_iota(jnp.int32, (4 * BLK, 1), 0)
    query_ids = segment((xl * 8 + c) * BLK + (row >> 6) * (2 * BLK) + row_of(row))
    bias_ref[...] = jnp.where(query_ids == key_ids, 0.0, -jnp.inf)


def attend_kernel(start_ref, bias_ref, qkv_ref, out_ref, ordered_ref):
    query = jnp.concatenate(
        [qkv_ref[pl.ds(pl.multiple_of(start_ref[y], BLK), BLK), 0:HD] for y in range(4)], axis=0
    )
    scores = lax.dot_general(
        query,
        qkv_ref[:, HD : 2 * HD],
        (((1,), (1,)), ((), ())),
        preferred_element_type=jnp.float32,
    ) * (HD**-0.5)
    scores = scores + bias_ref[...]
    weights = jnp.exp(scores - jnp.max(scores, axis=-1, keepdims=True))
    weights = (weights * (1.0 / jnp.sum(weights, axis=-1, keepdims=True))).astype(jnp.bfloat16)
    attended = jnp.dot(weights, qkv_ref[:, 2 * HD : 3 * HD], preferred_element_type=jnp.float32)
    for at in range(0, 4 * BLK, NZ):
        first = at // HALF * HALF + (at // NZ) % 2
        ordered_ref[pl.ds(first, NZ, stride=2), :] = attended[at : at + NZ]
    for y in range(4):
        out_ref[y] = ordered_ref[y * BLK : (y + 1) * BLK].astype(jnp.bfloat16)


def whole(memory=pltpu.VMEM):
    return pl.BlockSpec(memory_space=memory)


def call(kernel, out, in_specs, scratch=(), cost=(0, 10**6, 0), out_specs=None):
    flops, bytes_accessed, transcendentals = cost
    return pl.pallas_call(
        kernel,
        out_shape=out,
        in_specs=in_specs,
        out_specs=out_specs or jax.tree.map(lambda _: whole(), out),
        scratch_shapes=list(scratch),
        compiler_params=pltpu.CompilerParams(vmem_limit_bytes=VMEM_BYTES),
        cost_estimate=pl.CostEstimate(
            flops=flops, bytes_accessed=bytes_accessed, transcendentals=transcendentals
        ),
    )


def shards(patches, image_lengths, destination, weight):
    half_type = jnp.bfloat16

    slots = call(
        spread_kernel,
        jax.ShapeDtypeStruct((8, PIECE, QKV), half_type),
        [whole(pl.ANY)],
        [pltpu.SemaphoreType.DMA((8,))],
        out_specs=whole(pl.ANY),
    )(weight.reshape(PIECE, QKV))
    near = lax.all_gather(patches, ("xl", "c"), axis=0)
    slots, near = lax.optimization_barrier((slots, near))
    weight_set = lax.all_to_all(slots, ("y", "xh"), 0, 0, tiled=True)

    rows = call(
        column_kernel, jax.ShapeDtypeStruct((4 * LOCAL, KSET), half_type), [whole()]
    )(near)
    rows = lax.all_gather(rows, "z", axis=0, tiled=True)

    keep, give = call(
        project_kernel,
        (
            jax.ShapeDtypeStruct((ROWS, 2 * QKV), jnp.float32),
            jax.ShapeDtypeStruct((ROWS, 2 * QKV), jnp.float32),
        ),
        [whole(), whole()],
        [pltpu.VMEM((3, 4 * LOCAL * (NZ + 1), HD), jnp.float32)],
        cost=(10**9, 4 * 10**6, 0),
    )(rows, weight_set.reshape(4, 2, PIECE, QKV))

    got = lax.ppermute(give, "c", [(0, 1), (1, 0)])
    spread = call(
        pair_kernel,
        jax.ShapeDtypeStruct((4, NPACK * HALF, QKV), jnp.float32),
        [whole(), whole()],
    )(keep, got)
    parts = lax.all_to_all(spread, ("xl", "xh"), 0, 0, tiled=True)
    spread = call(total_kernel, jax.ShapeDtypeStruct((8, BLK, QKV), half_type), [whole()])(parts)
    blocks = lax.all_to_all(spread, ("xl", "y"), 0, 0, tiled=True)
    blocks = lax.all_gather(blocks.reshape(8 * BLK, QKV), "c", axis=0, tiled=True)

    bias, starts = call(
        mask_kernel,
        (
            jax.ShapeDtypeStruct((4 * BLK, NBLK * BLK), jnp.float32),
            jax.ShapeDtypeStruct((4,), jnp.int32),
        ),
        [whole(pltpu.SMEM)] * 2,
        cost=(10**6, 10**6, 0),
        out_specs=(whole(), whole(pltpu.SMEM)),
    )(destination, image_lengths)
    attended = call(
        attend_kernel,
        jax.ShapeDtypeStruct((4, BLK, HD), half_type),
        [whole(pltpu.SMEM), whole(), whole()],
        [pltpu.VMEM((4 * BLK + 8, HD), jnp.float32)],
        cost=(2 * 10**8, 10**6, 3 * 10**5),
    )(starts, bias, blocks)

    home = lax.all_to_all(attended, "y", 0, 0, tiled=True)
    return home[:NPACK].reshape(NPACK, BLK, 1, HD)


def solution(mesh):
    names, sizes = zip(*FINE)
    fine = Mesh(mesh.devices.reshape(sizes), names)
    return jax.shard_map(
        shards,
        mesh=fine,
        in_specs=(P(None, GROUP + SHARD, None), P(), P(), P(GROUP, SHARD, None)),
        out_specs=P(None, GROUP, SHARD, None),
        check_vma=False,
    )
```

```python
import jax
import jax.numpy as jnp
from jax import lax
from jax.experimental import pallas as pl
from jax.experimental.pallas import tpu as pltpu
from jax.sharding import Mesh, PartitionSpec as P

D = 5120
HD = 128
BLK = 64
HALF = BLK // 2
NPACK = 3
IMGS = 4
NBLK = 16
QKV = 3 * HD
NZ = 16
PIECE = D // 16
KSET = 4 * PIECE
LOCAL = NPACK * 2
ROWS = NPACK * BLK

FINE = (("xl", 2), ("y", 4), ("c", 2), ("xh", 2), ("z", 16))
GROUP = ("xl", "y", "c")
SHARD = ("xh", "z")
PACK_OF = (0, 1, 2, 2)
VMEM_BYTES = 32 * 2**20


def spread_kernel(w_ref, out_ref, sems):
    copies = [pltpu.make_async_copy(w_ref, out_ref.at[m], sems.at[m]) for m in range(8)]
    for copy in copies:
        copy.start()
    for copy in copies:
        copy.wait()


def column_kernel(x_ref, out_ref):
    own_xl, own_c = lax.axis_index("xl") == 1, lax.axis_index("c") == 1
    x = x_ref[...].astype(jnp.float32)
    x = jnp.where(own_xl, x[..., D // 2 :], x[..., : D // 2])
    x = jnp.concatenate([x[k, p] for k in range(4) for p in range(NPACK)], axis=0)
    cut = [
        jnp.where(own_c, x[:, (2 * y + 1) * PIECE : (2 * y + 2) * PIECE], x[:, 2 * y * PIECE : (2 * y + 1) * PIECE])
        for y in range(4)
    ]
    out_ref[...] = jnp.concatenate(cut, axis=1).astype(jnp.bfloat16)


def project_kernel(x_ref, w_ref, keep_ref, give_ref, product_ref):
    own = lax.axis_index("c")
    both = jnp.concatenate([w_ref[:, head].reshape(KSET, QKV) for head in range(2)], axis=1)
    product = jnp.dot(x_ref[...], both, preferred_element_type=jnp.float32)
    for k in range(6):
        product_ref[k, : 4 * LOCAL * NZ] = product[:, k * HD : (k + 1) * HD]
        columns = slice(k * HD, (k + 1) * HD)
        for p in range(NPACK):
            for xl in range(2):
                for i in range(2):
                    at = p * BLK + xl * HALF + i * NZ
                    first = xl * 2 * LOCAL + p * 2 + i
                    mine = product_ref[k, pl.ds(first + own * LOCAL, NZ, stride=4 * LOCAL), :]
                    theirs = product_ref[k, pl.ds(first + (1 - own) * LOCAL, NZ, stride=4 * LOCAL), :]
                    keep_ref[at : at + NZ, columns] = mine
                    give_ref[at : at + NZ, columns] = theirs


def pair_kernel(keep_ref, got_ref, out_ref):
    for p in range(NPACK):
        for xl in range(2):
            start = p * BLK + xl * HALF
            for head in range(2):
                columns = slice(head * QKV, (head + 1) * QKV)
                total = keep_ref[start : start + HALF, columns] + got_ref[start : start + HALF, columns]
                out_ref[xl * 2 + head, p * HALF : (p + 1) * HALF] = total


def total_kernel(parts_ref, out_ref):
    for p in range(NPACK):
        at = slice(p * HALF, (p + 1) * HALF)
        for xh in range(2):
            total = (parts_ref[xh, at] + parts_ref[2 + xh, at]).astype(jnp.bfloat16)
            for y, pack in enumerate(PACK_OF):
                if pack == p:
                    for xl in range(2):
                        out_ref[xl * 4 + y, xh * HALF : (xh + 1) * HALF] = total


def row_of(at):
    return (at & HALF) + ((at & (NZ - 1)) << 1) + ((at >> 4) & 1)


def attend_kernel(destination_ref, lengths_ref, qkv_ref, out_ref, ordered_ref):
    xl, y_own, c = (lax.axis_index(a) for a in ("xl", "y", "c"))
    pack = jnp.minimum(y_own, NPACK - 1)
    ends = []
    end = 0
    for i in range(IMGS):
        end = end + lengths_ref[pack, i]
        ends.append(end)

    def segment(position):
        count = jnp.zeros(position.shape, jnp.int32)
        for e in ends:
            count = count + (position >= e).astype(jnp.int32)
        return count

    lane = lax.broadcasted_iota(jnp.int32, (1, NBLK * BLK), 1)
    key_block = jnp.zeros_like(lane)
    slots = []
    for j in range(NBLK):
        slot = (j & 1) * 8 + (j >> 1)
        slots.append(slot)
        key_block = jnp.where((lane >> 6) == slot, destination_ref[pack, j], key_block)
    key_ids = segment(key_block * BLK + row_of(lane))

    queries = []
    for y in range(4):
        block = xl * 8 + y * 2 + c
        start = 0
        for j in range(NBLK):
            start = jnp.where(destination_ref[pack, j] == block, slots[j] * BLK, start)
        start = pl.multiple_of(start, BLK)
        queries.append(qkv_ref[pl.ds(start, BLK), 0:HD])
    query = jnp.concatenate(queries, axis=0)
    row = lax.broadcasted_iota(jnp.int32, (4 * BLK, 1), 0)
    query_ids = segment((xl * 8 + c) * BLK + (row >> 6) * (2 * BLK) + row_of(row))

    scores = lax.dot_general(
        query,
        qkv_ref[:, HD : 2 * HD],
        (((1,), (1,)), ((), ())),
        preferred_element_type=jnp.float32,
    ) * (HD**-0.5)
    scores = jnp.where(query_ids == key_ids, scores, -jnp.inf)
    weights = jnp.exp(scores - jnp.max(scores, axis=-1, keepdims=True))
    weights = (weights * (1.0 / jnp.sum(weights, axis=-1, keepdims=True))).astype(jnp.bfloat16)
    attended = jnp.dot(weights, qkv_ref[:, 2 * HD : 3 * HD], preferred_element_type=jnp.float32)
    for at in range(0, 4 * BLK, NZ):
        first = at // HALF * HALF + (at // NZ) % 2
        ordered_ref[pl.ds(first, NZ, stride=2), :] = attended[at : at + NZ]
    for y in range(4):
        out_ref[y] = ordered_ref[y * BLK : (y + 1) * BLK].astype(jnp.bfloat16)


def whole(memory=pltpu.VMEM):
    return pl.BlockSpec(memory_space=memory)


def call(kernel, out, in_specs, scratch=(), cost=(0, 10**6, 0), out_specs=None):
    flops, bytes_accessed, transcendentals = cost
    return pl.pallas_call(
        kernel,
        out_shape=out,
        in_specs=in_specs,
        out_specs=out_specs or jax.tree.map(lambda _: whole(), out),
        scratch_shapes=list(scratch),
        compiler_params=pltpu.CompilerParams(vmem_limit_bytes=VMEM_BYTES),
        cost_estimate=pl.CostEstimate(
            flops=flops, bytes_accessed=bytes_accessed, transcendentals=transcendentals
        ),
    )


def shards(patches, image_lengths, destination, weight):
    half_type = jnp.bfloat16

    slots = call(
        spread_kernel,
        jax.ShapeDtypeStruct((8, PIECE, QKV), half_type),
        [whole(pl.ANY)],
        [pltpu.SemaphoreType.DMA((8,))],
        out_specs=whole(pl.ANY),
    )(weight.reshape(PIECE, QKV))
    near = lax.all_gather(patches, ("xl", "c"), axis=0)
    slots, near = lax.optimization_barrier((slots, near))
    weight_set = lax.all_to_all(slots, ("y", "xh"), 0, 0, tiled=True)

    rows = call(
        column_kernel, jax.ShapeDtypeStruct((4 * LOCAL, KSET), half_type), [whole()]
    )(near)
    rows = lax.all_gather(rows, "z", axis=0, tiled=True)

    keep, give = call(
        project_kernel,
        (
            jax.ShapeDtypeStruct((ROWS, 2 * QKV), jnp.float32),
            jax.ShapeDtypeStruct((ROWS, 2 * QKV), jnp.float32),
        ),
        [whole(), whole()],
        [pltpu.VMEM((6, 4 * LOCAL * (NZ + 1), HD), jnp.float32)],
        cost=(10**9, 4 * 10**6, 0),
    )(rows, weight_set.reshape(4, 2, PIECE, QKV))

    got = lax.ppermute(give, "c", [(0, 1), (1, 0)])
    spread = call(
        pair_kernel,
        jax.ShapeDtypeStruct((4, NPACK * HALF, QKV), jnp.float32),
        [whole(), whole()],
    )(keep, got)
    parts = lax.all_to_all(spread, ("xl", "xh"), 0, 0, tiled=True)
    spread = call(total_kernel, jax.ShapeDtypeStruct((8, BLK, QKV), half_type), [whole()])(parts)
    blocks = lax.all_to_all(spread, ("xl", "y"), 0, 0, tiled=True)
    blocks = lax.all_gather(blocks.reshape(8 * BLK, QKV), "c", axis=0, tiled=True)

    attended = call(
        attend_kernel,
        jax.ShapeDtypeStruct((4, BLK, HD), half_type),
        [whole(pltpu.SMEM)] * 2 + [whole()],
        [pltpu.VMEM((4 * BLK + 8, HD), jnp.float32)],
        cost=(2 * 10**8, 10**6, 3 * 10**5),
    )(destination, image_lengths, blocks)

    home = lax.all_to_all(attended, "y", 0, 0, tiled=True)
    return home[:NPACK].reshape(NPACK, BLK, 1, HD)


def solution(mesh):
    names, sizes = zip(*FINE)
    fine = Mesh(mesh.devices.reshape(sizes), names)
    return jax.shard_map(
        shards,
        mesh=fine,
        in_specs=(P(None, GROUP + SHARD, None), P(), P(), P(GROUP, SHARD, None)),
        out_specs=P(None, GROUP, SHARD, None),
        check_vma=False,
    )
```
